512 devices in a mesh: dp: 16 (over y, z_hi), mod: 32 (over x, z_lo, core).
Axes of the slice: x: 4, y: 4, z: 16 (z_hi: 4, z_lo: 4; z = z_hi * 4 + z_lo), core: 2. Of those that a mesh axis runs over, the one named last changes fastest.
Arguments:
- normed_states: bfloat16 [65536, 8192], P(('dp', 'mod')), may hold values from -6 to 6
- kv_cotangent: bfloat16 [65536, 512], P(('dp', 'mod')), may hold values from -6 to 6
- token_types: int32 [65536, 1], P(('dp', 'mod')), may hold values from 0 to 1; in each aligned block of 128 rows (0 to 127, 128 to 255, ...) at most 96 rows name the same one
- kv_weight: bfloat16 [16384, 512], P('mod'), may hold values from -0.25 to 0.25
Outputs:
- state_grad: bfloat16 [65536, 8192], P(('dp', 'mod'))
- kv_weight_grad: float32 [16384, 512], P(('mod', 'dp'))
The draws below stay inside these ranges and needn't reach their ends.
Inputs may be any that keep to these rules, and one draw needn't show every extreme that they name: `token_types`: in each aligned block of 128 rows (the rows of one device) at most 96 rows name the same modality; in every draw some block has exactly 96 rows of one modality.
All inputs are finite; a program needn't handle non-finite values.
Results may differ from the reference program's by a relative error of at most 0.001.
Values may be sent and summed in bfloat16 or wider, within the bound.
A program may use at most 128 MiB of HBM per device.

```python
import math
import jax
import jax.numpy as jnp
import numpy as np
from jax import lax

D = 8192
KVW = 512
TOK_DEV = 128
CAP = 96
TOKENS = 65536
N_DP = 16
N_MOD = 32


def block_scale(key, shape, pieces, low, largest):
    level, own = 1.0, jax.random.fold_in(key, 6)
    for axis_at, parts in pieces:
        steps = jnp.exp(jax.random.uniform(jax.random.fold_in(own, axis_at), (parts,), jnp.float32, low / len(pieces), largest / len(pieces)))
        level = level * jnp.repeat(steps, shape[axis_at] // parts).reshape([-1 if axis == axis_at else 1 for axis in range(len(shape))])
    return level


def shared_out(rng, own, number, rows, count, top, limit, skew):
    sequence = jax.random.permutation(rng, count)
    heavy_load, ordinary = load_shares(count, rows * top, limit, skew, True), load_shares(count, rows * top, limit, skew, False)
    places = jnp.arange(count)

    def named(tallies, rotation):
        used = int((tallies > 0).sum())
        fixed = max(1, used // 4)
        shifted = fixed + (places - fixed + rotation * (used - fixed)) % max(1, count - fixed)
        return jnp.zeros((count,), jnp.int32).at[sequence[jnp.where(places < fixed, places, shifted)]].set(jnp.asarray(tallies, jnp.int32))

    tallies = jnp.where(number % 4 == 0, named(heavy_load, number // 4), named(ordinary, number - number // 4 - 1))
    mixed = jax.random.permutation(jax.random.fold_in(own, 3), count)
    donor, taker = mixed[0:count // 2 * 2:2], mixed[1:count // 2 * 2:2]
    margin = jnp.minimum(tallies[donor] - 1, limit - tallies[taker]) // 2
    margin = jnp.where((donor == sequence[0]) | (taker == sequence[0]) | (tallies[taker] == 0), 0, jnp.maximum(margin, 0))
    shifted = jax.random.randint(jax.random.fold_in(own, 4), (count // 2,), 0, 1 << 20) % (margin + 1)
    tallies = tallies.at[donor].add(-shifted).at[taker].add(shifted)
    items = jnp.searchsorted(jnp.cumsum(tallies), jnp.arange(rows * top), side="right").astype(jnp.int32)
    grid = items.reshape(top, rows).T
    grid = grid[jax.random.permutation(jax.random.fold_in(own, 1), rows)]
    rotation = jax.random.randint(jax.random.fold_in(own, 2), (rows, 1), 0, top)
    return jnp.take_along_axis(grid, (jnp.arange(top)[None, :] + rotation) % top, axis=1)


def load_shares(amount, total, limit, slope, full):
    weights = [(1 << 20) // math.isqrt(grade ** slope) + 1 for grade in range(1, amount + 1)]
    largest = limit if full else min(limit, max(-(-total // amount), total * weights[0] // sum(weights)))
    least = 1 if total - largest >= amount - 1 else 0
    counts, rest = [largest] + [least] * (amount - 1), total - largest - least * (amount - 1)
    while rest > 0:
        free = [i for i in range(1, amount) if counts[i] < largest] or [i for i in range(1, amount) if counts[i] < limit]
        mass, budget = sum([weights[i] for i in free]), rest
        for i in free:
            extra = min(limit - counts[i], max(1, budget * weights[i] // mass), rest)
            counts[i] = counts[i] + extra
            rest = rest - extra
    return np.array(counts)


def scatter_about(key, extent, deviation, bound, shards=(), held_as=jnp.bfloat16):
    values = jax.random.normal(key, extent, jnp.float32) * deviation
    if len(shards) > 0:
        values = block_scale(key, extent, shards, -0.22, 0.18) * values
    return jnp.clip(values, min=-bound, max=bound).astype(held_as)


def setup_inputs(seed: int = 0) -> dict:
    arg_keys = jax.random.split(jax.random.key(seed), 5)
    normed_states = scatter_about(arg_keys[0], (TOKENS, D), 1.0, 6.0, ((0, 512),))
    kv_cotangent = scatter_about(arg_keys[1], (TOKENS, KVW), 1.0, 6.0, ((0, 512),))
    token_types_keys = jax.random.split(jax.random.fold_in(arg_keys[2], 1), TOKENS // TOK_DEV)
    token_types_turns = jax.random.permutation(jax.random.fold_in(arg_keys[2], 3), TOKENS // TOK_DEV)
    token_types = jax.vmap(lambda own, number: shared_out(jax.random.fold_in(arg_keys[2], 2), own, number, TOK_DEV, 2, 1, CAP, 2))(token_types_keys, token_types_turns).reshape((TOKENS, 1))
    kv_weight = scatter_about(arg_keys[3], (2 * D, KVW), KVW ** -0.5, 0.25, ((0, 32),))
    return dict(normed_states=normed_states, kv_cotangent=kv_cotangent, token_types=token_types, kv_weight=kv_weight)


def reference(normed_states, kv_cotangent, token_types, kv_weight):
    row_kind = token_types[:, 0]
    text_mask = (row_kind == 0)[:, None]
    text_grads = jnp.where(text_mask, kv_cotangent, jnp.zeros_like(kv_cotangent))
    image_grads = jnp.where(text_mask, jnp.zeros_like(kv_cotangent), kv_cotangent)
    w_text = kv_weight[:D]
    w_image = kv_weight[D:]
    contract_cols = (((1,), (1,)), ((), ()))
    state_grad = (lax.dot_general(text_grads, w_text, contract_cols, preferred_element_type=jnp.float32) + lax.dot_general(image_grads, w_image, contract_cols, preferred_element_type=jnp.float32)).astype(jnp.bfloat16)
    group_rows = TOK_DEV * N_MOD
    contract_rows = (((0,), (0,)), ((), ()))

    def add_group(group, total):
        start = (group * group_rows).astype(jnp.int32)
        states = lax.dynamic_slice_in_dim(normed_states, start, group_rows, 0)
        text_part = lax.dynamic_slice_in_dim(text_grads, start, group_rows, 0)
        image_part = lax.dynamic_slice_in_dim(image_grads, start, group_rows, 0)
        upper = lax.dot_general(states, text_part, contract_rows, preferred_element_type=jnp.float32)
        lower = lax.dot_general(states, image_part, contract_rows, preferred_element_type=jnp.float32)
        stacked = jnp.concatenate([upper, lower], 0)
        return total + stacked
    summed = lax.fori_loop(0, N_DP, add_group, jnp.zeros((2 * D, kv_weight.shape[1]), jnp.float32))
    kv_weight_grad = summed * (1.0 / math.sqrt(TOKENS))
    return (state_grad, kv_weight_grad)
```

```python
import functools

import jax
import jax.numpy as jnp
from jax import lax
from jax.experimental import pallas as pl
from jax.experimental.pallas import tpu as pltpu
from jax.sharding import PartitionSpec as P

MESH = pl.DeviceIdType.MESH
F32, BF16 = jnp.float32, jnp.bfloat16
ROWS, WIDTH, KV = 128, 8192, 512
HALF, QUARTER = ROWS // 2, ROWS // 4
GROUP = 8 * ROWS
ZL, ZH, NZ = 4, 4, 16

DIRS = (
    (1, 0, 0, HALF, 128),
    (-1, 0, HALF, HALF, 192),
    (0, 1, 0, HALF, 256),
    (0, -1, HALF, HALF, 320),
    (1, 1, 0, QUARTER, 384),
    (1, -1, QUARTER, QUARTER, 416),
    (-1, 1, 2 * QUARTER, QUARTER, 448),
    (-1, -1, 3 * QUARTER, QUARTER, 480),
)
ITEMS = ((0, 0, 1, 0, ROWS, 512, 1),) + tuple(
    (dx, dy, dc, row, rows, dc * 512 + slot, abs(dx) * 4 + abs(dy) * 2 + dc)
    for dx, dy, row, rows, slot in DIRS
    for dc in (0, 1)
)


def kernel(
    x_ref, k_ref, t_ref, w_ref, dx_ref, dw_ref,
    xs, xr, kr, k2, wr, part, down, up, dxs, dxr, last, total,
    stage_sem, x_send, x_recv, k_send, k_recv, w_send, w_recv, d_send, d_recv,
    c_send, c_recv, l_send, l_recv, local_sem, out_sem,
):
    dp, mod = lax.axis_index("dp"), lax.axis_index("mod")
    y, zh = lax.div(dp, 4), lax.rem(dp, 4)
    x, zl, c = lax.div(mod, 8), lax.rem(lax.div(mod, 2), 4), lax.rem(mod, 2)
    z = zh * 4 + zl
    px, py, jy = lax.rem(x, 2), lax.rem(y, 2), lax.div(y, 2)

    def device(dx, dy, dz, dc):
        xx, yy = lax.rem(x + dx + 4, 4), lax.rem(y + dy + 4, 4)
        zz, cc = lax.rem(z + dz + NZ, NZ), lax.rem(c + dc, 2)
        return (yy * 4 + lax.div(zz, 4), xx * 8 + lax.rem(zz, 4) * 2 + cc)

    def column(rel, l, j):
        xx, yy = lax.rem(px + rel // 4, 2), lax.rem(py + (rel // 2) % 2, 2)
        cc = lax.rem(c + rel % 2, 2)
        return pl.multiple_of(xx * 4096 + l * 1024 + cc * 512 + yy * 128 + j * 256, 128)

    def remote(src, dst, send, recv, to):
        return pltpu.make_async_remote_copy(
            src_ref=src, dst_ref=dst, send_sem=send, recv_sem=recv,
            device_id=to, device_id_type=MESH,
        )

    for rel in (4, 5, 2, 3, 6, 7, 1, 0):
        for l in range(ZL):
            for j in range(2):
                lanes = pl.ds(j * 128, 128)
                dst = xr.at[l, pl.ds(0, ROWS), lanes] if rel == 0 else xs.at[rel - 1, l, :, lanes]
                pltpu.make_async_copy(
                    x_ref.at[:, pl.ds(column(rel, l, j), 128)], dst, stage_sem.at[rel]
                ).start()
    kr[0:ROWS, 0:KV] = k_ref[...]
    kr[0:ROWS, KV:] = jnp.broadcast_to(t_ref[...].astype(F32), (ROWS, 128)).astype(BF16)

    barrier = pltpu.get_barrier_semaphore()
    greeted = [(dx, dy, 0, dc) for dx, dy, dc, *_ in ITEMS]
    greeted += [(0, 0, 1, 0), (0, 0, -1, 0), (0, 0, 2, 0), (0, 0, -2, 0)]
    greeted += [(2, 0, 0, 0), (0, 2, 0, 0), (2, 2, 0, 0)]
    for offsets in greeted:
        pl.semaphore_signal(barrier, inc=1, device_id=device(*offsets), device_id_type=MESH)
    pl.semaphore_wait(barrier, len(greeted))

    k_copies = []
    for i, (dx, dy, row, rows, slot) in enumerate(DIRS):
        copy = remote(
            kr.at[pl.ds(row, rows)], kr.at[pl.ds(slot, rows)], k_send.at[i], k_recv.at[i], device(dx, dy, 0, 0)
        )
        copy.start()
        k_copies.append(copy)
    k_own = remote(
        kr.at[pl.ds(0, ROWS)], kr.at[pl.ds(512, ROWS)], k_send.at[8], k_recv.at[8], device(0, 0, 0, 1)
    )
    k_own.start()
    w_copies = []
    for i, (dz, j) in enumerate(((1, 0), (1, 1), (-1, 0), (-1, 1), (2, 0), (-2, 1))):
        rows = w_ref.at[pl.ds(pl.multiple_of((py + 2 * j) * 128, 128), 128)]
        copy = remote(rows, wr.at[0, zl, j], w_send.at[i], w_recv.at[i], device(0, 0, dz, 0))
        copy.start()
        w_copies.append((copy, i, lax.rem(zl + NZ - dz, 4), j))
    for j in range(2):
        rows = w_ref.at[pl.ds(pl.multiple_of((py + 2 * j) * 128, 128), 128)]
        pltpu.make_async_copy(rows, wr.at[0, zl, j], local_sem.at[j]).start()
    staged = set()
    x_copies = []
    for i in list(range(1, len(ITEMS))) + [0]:
        dx, dy, dc, row, rows, slot, rel = ITEMS[i]
        if rel not in staged:
            staged.add(rel)
            pltpu.make_async_copy(xs.at[rel - 1], xs.at[rel - 1], stage_sem.at[rel]).wait()
        copy = remote(
            xs.at[rel - 1, :, pl.ds(row, rows)], xr.at[:, pl.ds(slot, rows)],
            x_send.at[i], x_recv.at[i], device(dx, dy, 0, dc),
        )
        copy.start()
        x_copies.append(copy)
    mine = xr.at[:, pl.ds(0, ROWS)]
    pltpu.make_async_copy(mine, mine, stage_sem.at[0]).wait()

    for copy in k_copies:
        copy.wait_recv()
    relay = remote(
        kr.at[pl.ds(128, 384)], kr.at[pl.ds(640, 384)], k_send.at[9], k_recv.at[9], device(0, 0, 0, 1)
    )
    relay.start()
    k_own.wait_recv()
    relay.wait_recv()
    own_kind = lax.div(x, 2).astype(F32)
    for i in range(8):
        rows = pl.ds(i * 128, 128)
        kind = kr[rows, KV:].astype(F32)
        mask = 1.0 - jnp.abs(kind - own_kind)
        mask = jnp.concatenate([mask] * 4, 1)
        values = kr[rows, 0:KV].astype(F32)
        k2[rows, 0:KV] = (values * mask).astype(BF16)
        k2[rows, KV:] = (values * (1.0 - mask)).astype(BF16)

    for copy, i, l, j in w_copies:
        here = wr.at[0, l, j]
        pltpu.make_async_copy(here, here, w_recv.at[i]).wait()
    for j in range(2):
        here = wr.at[0, zl, j]
        pltpu.make_async_copy(here, here, local_sem.at[j]).wait()
    wx_copies = []
    for l in range(ZL):
        copy = remote(
            wr.at[0, l, jy], wr.at[1, l, jy], w_send.at[6 + l], w_recv.at[6 + l], device(2, 0, 0, 0)
        )
        copy.start()
        wx_copies.append(copy)

    for copy in x_copies:
        copy.wait_recv()
    for l in range(ZL):
        for half in range(2):
            lanes = pl.ds(half * KV, KV)
            value = lax.dot_general(
                xr[l], k2[:, lanes], (((0,), (0,)), ((), ())), preferred_element_type=F32
            )
            part[l, :, :, :, lanes] = value.reshape(2, ZH, 32, KV)

    def chunk(target):
        target = lax.rem(target + NZ, NZ)
        return lax.rem(target, 4), lax.div(target, 4)

    chains = []

    def chain(step):
        for at, (buffer, dz, target, count) in enumerate(
            ((down, -1, z + 8 + step, 8), (up, 1, z + 7 - step, 7))
        ):
            if step >= count:
                continue
            l, h = chunk(target)
            if step == 0:
                src = part.at[l, :, h]
            else:
                chains[2 * (step - 1) + at].wait_recv()
                src = buffer.at[step - 1]
                src[...] = src[...] + part[l, :, h]
            i = at * 8 + step
            copy = remote(src, buffer.at[step], c_send.at[i], c_recv.at[i], device(0, 0, dz, 0))
            copy.start()
            chains.append(copy)

    wy_copies = []

    def weights_y():
        for l in range(ZL):
            wx_copies[l].wait_recv()
            copy = remote(
                wr.at[1, l, jy], wr.at[1, l, jy], w_send.at[10 + l], w_recv.at[10 + l], device(0, 2, 0, 0)
            )
            copy.start()
            wy_copies.append(copy)

    d_copies = []

    def state_grad(l):
        here = wr.at[1, l, 1 - jy]
        pltpu.make_async_copy(here, here, w_recv.at[10 + l]).wait()
        own, other = wr[0, l].reshape(256, KV), wr[1, l].reshape(256, KV)
        for half in range(2):
            rows = pl.ds(half * 512, 512)
            dims = (((1,), (1,)), ((), ()))
            value = lax.dot_general(k2[rows, 0:KV], own, dims, preferred_element_type=F32)
            value += lax.dot_general(k2[rows, KV:], other, dims, preferred_element_type=F32)
            dxs[l, rows] = value.astype(BF16)
        for i, (dx, dy, dc, row, rows, slot, rel) in enumerate(ITEMS):
            copy = remote(
                dxs.at[l, pl.ds(slot, rows)], dxr.at[rel - 1, l, pl.ds(row, rows)],
                d_send.at[l, i], d_recv.at[l, i], device(-dx, -dy, 0, dc),
            )
            copy.start()
            d_copies.append(copy)
        for j in range(2):
            lanes = pl.ds(j * 128, 128)
            pltpu.make_async_copy(
                dxs.at[l, pl.ds(0, ROWS), lanes], dx_ref.at[:, pl.ds(column(0, l, j), 128)], out_sem.at[0]
            ).start()

    chain(0)
    weights_y()
    chain(1)
    chain(2)
    for l in range(ZL):
        state_grad(l)
        chain(3 + l)
    chain(7)

    chains[15 - 1].wait_recv()
    chains[13].wait_recv()
    total[...] = part[zl, :, zh] + down[7] + up[6]
    l_copies = []
    for i, (dx, dy, j, first) in enumerate(
        ((2, 0, jy, KV), (0, 2, 1 - jy, 0), (2, 2, 1 - jy, KV))
    ):
        copy = remote(
            total.at[j, :, pl.ds(first, KV)], last.at[i], l_send.at[i], l_recv.at[i], device(dx, dy, 0, 0)
        )
        copy.start()
        l_copies.append(copy)

    for copy in d_copies:
        copy.wait_recv()
    for rel in range(1, 8):
        for l in range(ZL):
            for j in range(2):
                pltpu.make_async_copy(
                    dxr.at[rel - 1, l, :, pl.ds(j * 128, 128)],
                    dx_ref.at[:, pl.ds(column(rel, l, j), 128)],
                    out_sem.at[0],
                ).start()
    for copy in l_copies:
        copy.wait_recv()
    dw_ref[...] = (total[jy, :, 0:KV] + last[0] + last[1] + last[2]) * (1.0 / 256.0)

    pltpu.make_async_copy(dx_ref, dx_ref, out_sem.at[0]).wait()
    for copy in k_copies + [k_own, relay] + x_copies + wx_copies + wy_copies + chains + d_copies + l_copies:
        copy.wait_send()
    for copy, *_ in w_copies:
        copy.wait_send()


def body(normed_states, kv_cotangent, token_types, kv_weight):
    any_spec, vmem = pl.BlockSpec(memory_space=pl.ANY), pl.BlockSpec(memory_space=pltpu.VMEM)
    dma = pltpu.SemaphoreType.DMA
    return pl.pallas_call(
        kernel,
        out_shape=(
            jax.ShapeDtypeStruct((ROWS, WIDTH), BF16),
            jax.ShapeDtypeStruct((32, KV), F32),
        ),
        in_specs=[any_spec, vmem, vmem, vmem],
        out_specs=(any_spec, vmem),
        scratch_shapes=[
            pltpu.VMEM((7, ZL, ROWS, 256), BF16),
            pltpu.VMEM((ZL, GROUP, 256), BF16),
            pltpu.VMEM((GROUP, KV + 128), BF16),
            pltpu.VMEM((GROUP, 2 * KV), BF16),
            pltpu.VMEM((2, ZL, 2, 128, KV), BF16),
            pltpu.VMEM((ZL, 2, ZH, 32, 2 * KV), F32),
            pltpu.VMEM((8, 2, 32, 2 * KV), F32),
            pltpu.VMEM((7, 2, 32, 2 * KV), F32),
            pltpu.VMEM((ZL, GROUP, 256), BF16),
            pltpu.VMEM((7, ZL, ROWS, 256), BF16),
            pltpu.VMEM((3, 32, KV), F32),
            pltpu.VMEM((2, 32, 2 * KV), F32),
            dma((8,)),
            dma((len(ITEMS),)),
            dma((len(ITEMS),)),
            dma((10,)),
            dma((10,)),
            dma((14,)),
            dma((14,)),
            dma((ZL, len(ITEMS))),
            dma((ZL, len(ITEMS))),
            dma((16,)),
            dma((16,)),
            dma((3,)),
            dma((3,)),
            dma((2,)),
            dma((1,)),
        ],
        compiler_params=pltpu.CompilerParams(
            collective_id=0, has_side_effects=True, vmem_limit_bytes=48 * 2**20
        ),
        cost_estimate=pl.CostEstimate(flops=2**32, bytes_accessed=5 * 2**20, transcendentals=0),
        name="exchange",
    )(normed_states, kv_cotangent, token_types, kv_weight)


def solution(mesh):
    in_specs = (
        P(("dp", "mod"), None),
        P(("dp", "mod"), None),
        P(("dp", "mod"), None),
        P("mod", None),
    )
    out_specs = (P(("dp", "mod"), None), P(("mod", "dp"), None))
    return jax.shard_map(body, mesh=mesh, in_specs=in_specs, out_specs=out_specs, check_vma=False)
```

```python
import jax
import jax.numpy as jnp
from jax import lax
from jax.experimental import pallas as pl
from jax.experimental.pallas import tpu as pltpu
from jax.sharding import PartitionSpec as P

MESH = pl.DeviceIdType.MESH
F32, BF16, I16, I32 = jnp.float32, jnp.bfloat16, jnp.int16, jnp.int32
ROWS, WIDTH, KV = 128, 8192, 512
HALF, QUARTER = ROWS // 2, ROWS // 4
GROUP = 8 * ROWS
ZL, ZH, NZ = 4, 4, 16
UNIT = 16
TOP = 32767.0

DIRS = (
    (1, 0, 0, HALF, 128),
    (-1, 0, HALF, HALF, 192),
    (0, 1, 0, HALF, 256),
    (0, -1, HALF, HALF, 320),
    (1, 1, 0, QUARTER, 384),
    (1, -1, QUARTER, QUARTER, 416),
    (-1, 1, 2 * QUARTER, QUARTER, 448),
    (-1, -1, 3 * QUARTER, QUARTER, 480),
)
ITEMS = tuple(
    (dx, dy, dc, row, rows, dc * 512 + slot, abs(dx) * 4 + abs(dy) * 2 + dc)
    for dx, dy, row, rows, slot in DIRS
    for dc in (0, 1)
) + ((0, 0, 1, 0, ROWS, 512, 1),)
ALONG_Z = ((1, 0, 128, 1), (-1, 0, 128, 2), (2, 0, 64, 3), (-2, 64, 64, 3))


def kernel(
    x_ref, k_ref, t_ref, w_ref, dx_ref, dw_ref,
    xs, xr, kr, k2, kinds, wr, part, sums, units, dxs, dxr, last, total,
    stage_sem, x_send, x_recv, k_send, k_recv, w_send, w_recv, d_send, d_recv,
    c_send, c_recv, l_send, l_recv, local_sem, out_sem,
):
    dp, mod = lax.axis_index("dp"), lax.axis_index("mod")
    y, zh = lax.div(dp, 4), lax.rem(dp, 4)
    x, zl, c = lax.div(mod, 8), lax.rem(lax.div(mod, 2), 4), lax.rem(mod, 2)
    z = zh * 4 + zl
    px, py, jy = lax.rem(x, 2), lax.rem(y, 2), lax.div(y, 2)
    jn = 1 - jy

    def device(dx, dy, dz, dc):
        xx, yy = lax.rem(x + dx + 4, 4), lax.rem(y + dy + 4, 4)
        zz, cc = lax.rem(z + dz + NZ, NZ), lax.rem(c + dc, 2)
        return (yy * 4 + lax.div(zz, 4), xx * 8 + lax.rem(zz, 4) * 2 + cc)

    def column(rel, l, j):
        xx, yy = lax.rem(px + rel // 4, 2), lax.rem(py + (rel // 2) % 2, 2)
        cc = lax.rem(c + rel % 2, 2)
        return pl.multiple_of(xx * 4096 + l * 1024 + cc * 512 + yy * 128 + j * 256, 128)

    def remote(src, dst, send, recv, to):
        return pltpu.make_async_remote_copy(
            src_ref=src, dst_ref=dst, send_sem=send, recv_sem=recv,
            device_id=to, device_id_type=MESH,
        )

    def landed(ref, sem):
        pltpu.make_async_copy(ref, ref, sem).wait()

    barrier = pltpu.get_barrier_semaphore()
    greeted = [(dx, dy, 0, dc) for dx, dy, dc, *_ in ITEMS]
    greeted += [(0, 0, 1, 0), (0, 0, -1, 0), (0, 0, 2, 0), (0, 0, -2, 0)]
    greeted += [(2, 0, 0, 0), (0, 2, 0, 0), (2, 2, 0, 0)]
    for offsets in greeted:
        pl.semaphore_signal(barrier, inc=1, device_id=device(*offsets), device_id_type=MESH)

    k_in = pltpu.make_async_copy(k_ref, kr.at[pl.ds(0, ROWS), pl.ds(0, KV)], local_sem.at[0])
    k_in.start()
    t_in = pltpu.make_async_copy(t_ref, kinds, local_sem.at[1])
    t_in.start()
    for rel in (4, 5, 2, 3, 6, 7, 1):
        for l in range(ZL):
            for j in range(2):
                pltpu.make_async_copy(
                    x_ref.at[:, pl.ds(column(rel, l, j), 128)],
                    xs.at[rel - 1, j, :, pl.ds(l * 128, 128)],
                    stage_sem.at[rel],
                ).start()
    for o, j in enumerate((jn, jy)):
        for l in range(ZL):
            pltpu.make_async_copy(
                x_ref.at[:, pl.ds(column(0, l, j), 128)],
                xr.at[o, pl.ds(0, ROWS), pl.ds(l * 128, 128)],
                stage_sem.at[0],
            ).start()
    for r, j in enumerate((jy, jn)):
        rows = pl.ds(pl.multiple_of((py + 2 * j) * 128, 128), 128)
        pltpu.make_async_copy(w_ref.at[rows], wr.at[0, j, zl], local_sem.at[2 + r]).start()
    k_in.wait()
    t_in.wait()
    kr[0:ROWS, KV:] = jnp.broadcast_to(kinds[...].astype(F32), (ROWS, 128)).T.astype(BF16)

    pl.semaphore_wait(barrier, len(greeted))

    w_copies, d_copies, chains = [], [], {}
    blocks = [lax.rem(zl + 4 + d, 4) for d in (0, -1, 1, 2)]

    def w_along_z(r):
        j = (jy, jn, jy)[r]
        for i, (dz, row, rows, _) in enumerate(ALONG_Z):
            start = pl.multiple_of((py + 2 * j) * 128 + row, 64)
            dst = wr.at[r // 2, j, zl, pl.ds(row, rows)]
            copy = remote(
                dst if r == 2 else w_ref.at[pl.ds(start, rows)], dst,
                w_send.at[4 * r + i], w_recv.at[4 * r + i], device(0, 0, dz, 0),
            )
            copy.start()
            w_copies.append(copy)

    def w_arrived(r, q):
        j = (jy, jn, jy)[r]
        if q == 0 and r < 2:
            landed(wr.at[0, j, zl], local_sem.at[2 + r])
        for i, (_, row, rows, place) in enumerate(ALONG_Z):
            if place == q:
                landed(wr.at[r // 2, j, blocks[q], pl.ds(row, rows)], w_recv.at[4 * r + i])

    w_across = remote(
        w_ref.at[pl.ds(pl.multiple_of((py + 2 * jy) * 128, 128), 128)], wr.at[1, jy, zl],
        w_send.at[12], w_recv.at[12], device(2, 0, 0, 0),
    )

    def w_along_y(q):
        w_arrived(2, q)
        ref = wr.at[1, jy, blocks[q]]
        copy = remote(ref, ref, w_send.at[13 + q], w_recv.at[13 + q], device(0, 2, 0, 0))
        copy.start()
        w_copies.append(copy)

    def w_all(r):
        for q in range(4):
            w_arrived(r, q)
            if r == 1:
                landed(wr.at[1, jn, blocks[q]], w_recv.at[13 + q])

    k_copies = []
    for i, (dx, dy, row, rows, slot) in enumerate(DIRS):
        copy = remote(
            kr.at[pl.ds(row, rows)], kr.at[pl.ds(slot, rows)], k_send.at[i], k_recv.at[i], device(dx, dy, 0, 0)
        )
        copy.start()
        k_copies.append(copy)
    k_own = remote(
        kr.at[pl.ds(0, ROWS)], kr.at[pl.ds(512, ROWS)], k_send.at[8], k_recv.at[8], device(0, 0, 0, 1)
    )
    k_own.start()
    x_copies = ([], [])
    staged = set()
    for o in range(2):
        if o == 0:
            w_across.start()
            w_copies.append(w_across)
            w_along_z(0)
        for i, (dx, dy, dc, row, rows, slot, rel) in enumerate(ITEMS):
            if rel not in staged:
                staged.add(rel)
                landed(xs.at[rel - 1], stage_sem.at[rel])
            there = lax.div(lax.rem(y + dy + 4, 4), 2)
            copy = remote(
                xs.at[rel - 1, there if o else 1 - there, pl.ds(row, rows)],
                xr.at[o, pl.ds(slot, rows)],
                x_send.at[o, i], x_recv.at[o, i], device(dx, dy, 0, dc),
            )
            copy.start()
            x_copies[o].append(copy)
    landed(xr.at[:, pl.ds(0, ROWS)], stage_sem.at[0])

    w_across.wait_recv()
    w_along_z(2)
    w_along_z(1)
    for copy in k_copies:
        copy.wait_recv()
    relay = remote(
        kr.at[pl.ds(128, 384)], kr.at[pl.ds(640, 384)], k_send.at[9], k_recv.at[9], device(0, 0, 0, 1)
    )
    relay.start()
    k_own.wait_recv()
    own_kind = lax.div(x, 2).astype(F32)

    def masked(i):
        rows = pl.ds(i * 128, 128)
        mask = (1.0 - jnp.abs(kr[rows, KV:].astype(F32) - own_kind)).astype(BF16)
        values = kr[rows, 0:KV]
        own = values * jnp.concatenate([mask] * 4, 1)
        k2[rows, 0:KV] = own
        k2[rows, KV:] = values - own

    for i in range(5):
        masked(i)
    relay.wait_recv()
    for i in range(5, 8):
        masked(i)

    def partial(o):
        for copy in x_copies[o]:
            copy.wait_recv()
        for half in range(2):
            lanes = pl.ds(half * KV, KV)
            value = lax.dot_general(
                xr[o], k2[:, lanes], (((0,), (0,)), ((), ())), preferred_element_type=F32
            )
            part[o, :, :, :, lanes] = value.reshape(ZL, ZH, 32, KV)

    def state_grad(r, block):
        j = (jy, jn)[r]
        rows = pl.ds(block * 256, 256)
        dims = (((1,), (1,)), ((), ()))
        own, other = wr[0, j].reshape(512, KV), wr[1, j].reshape(512, KV)
        value = lax.dot_general(k2[rows, 0:KV], own, dims, preferred_element_type=F32)
        value += lax.dot_general(k2[rows, KV:], other, dims, preferred_element_type=F32)
        dxs[j, rows] = value.astype(BF16)
        for i, (dx, dy, dc, row, n, slot, rel) in enumerate(ITEMS):
            if slot // 256 != block:
                continue
            copy = remote(
                dxs.at[j, pl.ds(slot, n)], dxr.at[rel - 1, j, pl.ds(row, n)],
                d_send.at[r, i], d_recv.at[r, i], device(-dx, -dy, 0, dc),
            )
            copy.start()
            d_copies.append(copy)

    def chunk(target):
        target = lax.rem(target + NZ, NZ)
        return lax.rem(target, 4), lax.div(target, 4)

    def chain(step, o, half):
        rows = pl.ds(half * UNIT, UNIT)
        for at, (dz, target, count) in enumerate(((-1, z + 8 + step, 8), (1, z + 7 - step, 7))):
            if step >= count:
                continue
            if step > 0:
                for copy in chains[step - 1, o, half, at]:
                    copy.wait_recv()
            l, h = chunk(target)
            codes, scale = sums.at[at, step, o, half], units.at[at, step, o, half]
            value = part[o, l, h, rows]
            if step > 0:
                value += codes[...].astype(F32) * scale[0:1, 0:1]
            top = jnp.maximum(jnp.max(jnp.abs(value), keepdims=True), 1e-30)
            codes[...] = jnp.round(value * (TOP / top)).astype(I32).astype(I16)
            scale[...] = jnp.broadcast_to(top * (1.0 / TOP), (8, 128))
            to, copies = device(0, 0, dz, 0), []
            for i, ref in enumerate((units, sums)):
                copy = remote(
                    ref.at[at, step, o, half], ref.at[at, step + 1, o, half],
                    c_send.at[at, step, o, half, i], c_recv.at[at, step, o, half, i], to,
                )
                copy.start()
                copies.append(copy)
            chains[step, o, half, at] = copies

    partial(0)
    for half in range(2):
        chain(0, 0, half)
    partial(1)
    for half in range(2):
        chain(0, 1, half)
    for q in range(4):
        w_along_y(q)

    background = {
        (1, 0): lambda: (w_all(0), state_grad(0, 0)),
        (1, 2): lambda: state_grad(0, 1),
        (2, 0): lambda: state_grad(0, 2),
        (2, 2): lambda: state_grad(0, 3),
        (4, 0): lambda: (w_all(1), state_grad(1, 0)),
        (4, 2): lambda: state_grad(1, 1),
        (5, 0): lambda: state_grad(1, 2),
        (5, 2): lambda: state_grad(1, 3),
    }
    for step in range(1, 8):
        for unit in range(4):
            chain(step, unit // 2, unit % 2)
            if (step, unit) in background:
                background[step, unit]()

    l_copies = []
    for o in range(2):
        for half in range(2):
            rows = pl.ds(half * UNIT, UNIT)
            value = part[o, zl, zh, rows]
            for at, count in ((0, 8), (1, 7)):
                for copy in chains[count - 1, o, half, at]:
                    copy.wait_recv()
                value += sums[at, count, o, half].astype(F32) * units[at, count, o, half, 0:1, 0:1]
            total[o, rows] = value
        for i, dx, dy, first in (((0, 2, 2, KV), (1, 0, 2, 0)), ((2, 2, 0, KV),))[o]:
            copy = remote(
                total.at[o, :, pl.ds(first, KV)], last.at[i], l_send.at[i], l_recv.at[i], device(dx, dy, 0, 0)
            )
            copy.start()
            l_copies.append(copy)

    for copy in d_copies:
        copy.wait_recv()
    for rel in range(8):
        for l in range(ZL):
            for j in range(2):
                lanes = pl.ds(l * 128, 128)
                src = dxs.at[j, pl.ds(0, ROWS), lanes] if rel == 0 else dxr.at[rel - 1, j, :, lanes]
                pltpu.make_async_copy(src, dx_ref.at[:, pl.ds(column(rel, l, j), 128)], out_sem.at[0]).start()
    for copy in l_copies:
        copy.wait_recv()
    dw_ref[...] = (total[1, :, 0:KV] + last[0] + last[1] + last[2]) * (1.0 / 256.0)

    landed(dx_ref, out_sem.at[0])
    for copy in k_copies + [k_own, relay] + x_copies[0] + x_copies[1] + w_copies:
        copy.wait_send()
    for copy in d_copies + l_copies:
        copy.wait_send()
    for copies in chains.values():
        for copy in copies:
            copy.wait_send()


def body(normed_states, kv_cotangent, token_types, kv_weight):
    any_spec, vmem = pl.BlockSpec(memory_space=pl.ANY), pl.BlockSpec(memory_space=pltpu.VMEM)
    dma = pltpu.SemaphoreType.DMA
    return pl.pallas_call(
        kernel,
        out_shape=(
            jax.ShapeDtypeStruct((ROWS, WIDTH), BF16),
            jax.ShapeDtypeStruct((32, KV), F32),
        ),
        in_specs=[any_spec] * 4,
        out_specs=(any_spec, vmem),
        scratch_shapes=[
            pltpu.VMEM((7, 2, ROWS, KV), BF16),
            pltpu.VMEM((2, GROUP, KV), BF16),
            pltpu.VMEM((GROUP, KV + 128), BF16),
            pltpu.VMEM((GROUP, 2 * KV), BF16),
            pltpu.VMEM((1, ROWS), I32),
            pltpu.VMEM((2, 2, ZL, 128, KV), BF16),
            pltpu.VMEM((2, ZL, ZH, 32, 2 * KV), F32),
            pltpu.VMEM((2, 9, 2, 2, UNIT, 2 * KV), I16),
            pltpu.VMEM((2, 9, 2, 2, 8, 128), F32),
            pltpu.VMEM((2, GROUP, KV), BF16),
            pltpu.VMEM((7, 2, ROWS, KV), BF16),
            pltpu.VMEM((3, 32, KV), F32),
            pltpu.VMEM((2, 32, 2 * KV), F32),
            dma((8,)),
            dma((2, len(ITEMS))),
            dma((2, len(ITEMS))),
            dma((10,)),
            dma((10,)),
            dma((17,)),
            dma((17,)),
            dma((2, len(ITEMS))),
            dma((2, len(ITEMS))),
            dma((2, 8, 2, 2, 2)),
            dma((2, 8, 2, 2, 2)),
            dma((3,)),
            dma((3,)),
            dma((4,)),
            dma((1,)),
        ],
        compiler_params=pltpu.CompilerParams(
            collective_id=0, has_side_effects=True, vmem_limit_bytes=60 * 2**20
        ),
        cost_estimate=pl.CostEstimate(flops=2**32, bytes_accessed=5 * 2**20, transcendentals=0),
        name="exchange",
    )(normed_states, kv_cotangent, token_types.reshape(1, ROWS), kv_weight)


def solution(mesh):
    in_specs = (
        P(("dp", "mod"), None),
        P(("dp", "mod"), None),
        P(("dp", "mod"), None),
        P("mod", None),
    )
    out_specs = (P(("dp", "mod"), None), P(("mod", "dp"), None))
    return jax.shard_map(body, mesh=mesh, in_specs=in_specs, out_specs=out_specs, check_vma=False)
```

```python
import jax
import jax.numpy as jnp
from jax import lax
from jax.experimental import pallas as pl
from jax.experimental.pallas import tpu as pltpu
from jax.sharding import PartitionSpec as P

MESH = pl.DeviceIdType.MESH
F32, BF16, I16, I32 = jnp.float32, jnp.bfloat16, jnp.int16, jnp.int32
ROWS, WIDTH, KV = 128, 8192, 512
HALF, QUARTER = ROWS // 2, ROWS // 4
GROUP = 8 * ROWS
ZL, ZH, NZ = 4, 4, 16
UNIT = 16
TOP = 32767.0

DIRS = (
    (1, 0, 0, HALF, 128),
    (-1, 0, HALF, HALF, 192),
    (0, 1, 0, HALF, 256),
    (0, -1, HALF, HALF, 320),
    (1, 1, 0, QUARTER, 384),
    (1, -1, QUARTER, QUARTER, 416),
    (-1, 1, 2 * QUARTER, QUARTER, 448),
    (-1, -1, 3 * QUARTER, QUARTER, 480),
)
ITEMS = tuple(
    (dx, dy, dc, row, rows, dc * 512 + slot, abs(dx) * 4 + abs(dy) * 2 + dc)
    for dx, dy, row, rows, slot in DIRS
    for dc in (0, 1)
) + ((0, 0, 1, 0, ROWS, 512, 1),)
ALONG_Z = ((1, 0, 128, 1), (-1, 0, 128, 2), (2, 0, 64, 3), (-2, 64, 64, 3))


def kernel(
    x_ref, k_ref, t_ref, w_ref, dx_ref, dw_ref,
    xs, xr, kr, k2, kinds, wr, part, sums, units, dxs, dxr, last, total,
    stage_sem, x_send, x_recv, k_send, k_recv, w_send, w_recv, d_send, d_recv,
    c_send, c_recv, l_send, l_recv, local_sem, out_sem,
):
    dp, mod = lax.axis_index("dp"), lax.axis_index("mod")
    y, zh = lax.div(dp, 4), lax.rem(dp, 4)
    x, zl, c = lax.div(mod, 8), lax.rem(lax.div(mod, 2), 4), lax.rem(mod, 2)
    z = zh * 4 + zl
    px, py, jy = lax.rem(x, 2), lax.rem(y, 2), lax.div(y, 2)
    jn = 1 - jy

    def device(dx, dy, dz, dc):
        xx, yy = lax.rem(x + dx + 4, 4), lax.rem(y + dy + 4, 4)
        zz, cc = lax.rem(z + dz + NZ, NZ), lax.rem(c + dc, 2)
        return (yy * 4 + lax.div(zz, 4), xx * 8 + lax.rem(zz, 4) * 2 + cc)

    def column(rel, l, j):
        xx, yy = lax.rem(px + rel // 4, 2), lax.rem(py + (rel // 2) % 2, 2)
        cc = lax.rem(c + rel % 2, 2)
        return pl.multiple_of(xx * 4096 + l * 1024 + cc * 512 + yy * 128 + j * 256, 128)

    def remote(src, dst, send, recv, to):
        return pltpu.make_async_remote_copy(
            src_ref=src, dst_ref=dst, send_sem=send, recv_sem=recv,
            device_id=to, device_id_type=MESH,
        )

    def landed(ref, sem):
        pltpu.make_async_copy(ref, ref, sem).wait()

    barrier = pltpu.get_barrier_semaphore()
    greeted = [(dx, dy, 0, dc) for dx, dy, dc, *_ in ITEMS]
    greeted += [(0, 0, 1, 0), (0, 0, -1, 0), (0, 0, 2, 0), (0, 0, -2, 0)]
    greeted += [(2, 0, 0, 0), (0, 2, 0, 0), (2, 2, 0, 0)]
    for offsets in greeted:
        pl.semaphore_signal(barrier, inc=1, device_id=device(*offsets), device_id_type=MESH)

    k_in = pltpu.make_async_copy(k_ref, kr.at[pl.ds(0, ROWS), pl.ds(0, KV)], local_sem.at[0])
    k_in.start()
    t_in = pltpu.make_async_copy(t_ref, kinds, local_sem.at[1])
    t_in.start()
    for rel in (4, 5, 2, 3, 6, 7, 1):
        for l in range(ZL):
            for j in range(2):
                pltpu.make_async_copy(
                    x_ref.at[:, pl.ds(column(rel, l, j), 128)],
                    xs.at[rel - 1, j, :, pl.ds(l * 128, 128)],
                    stage_sem.at[rel],
                ).start()
    for o, j in enumerate((jn, jy)):
        for l in range(ZL):
            pltpu.make_async_copy(
                x_ref.at[:, pl.ds(column(0, l, j), 128)],
                xr.at[o, pl.ds(0, ROWS), pl.ds(l * 128, 128)],
                stage_sem.at[0],
            ).start()
    for r, j in enumerate((jy, jn)):
        rows = pl.ds(pl.multiple_of((py + 2 * j) * 128, 128), 128)
        pltpu.make_async_copy(w_ref.at[rows], wr.at[0, j, zl], local_sem.at[2 + r]).start()
    k_in.wait()
    t_in.wait()
    kr[0:ROWS, KV:] = jnp.broadcast_to(kinds[...].astype(F32), (ROWS, 128)).T.astype(BF16)

    pl.semaphore_wait(barrier, len(greeted))

    w_copies, d_copies, chains = [], [], {}
    blocks = [lax.rem(zl + 4 + d, 4) for d in (0, -1, 1, 2)]

    def w_along_z(r):
        j = (jy, jn, jy)[r]
        for i, (dz, row, rows, _) in enumerate(ALONG_Z):
            start = pl.multiple_of((py + 2 * j) * 128 + row, 64)
            dst = wr.at[r // 2, j, zl, pl.ds(row, rows)]
            copy = remote(
                dst if r == 2 else w_ref.at[pl.ds(start, rows)], dst,
                w_send.at[4 * r + i], w_recv.at[4 * r + i], device(0, 0, dz, 0),
            )
            copy.start()
            w_copies.append(copy)

    def w_arrived(r, q):
        j = (jy, jn, jy)[r]
        if q == 0 and r < 2:
            landed(wr.at[0, j, zl], local_sem.at[2 + r])
        for i, (_, row, rows, place) in enumerate(ALONG_Z):
            if place == q:
                landed(wr.at[r // 2, j, blocks[q], pl.ds(row, rows)], w_recv.at[4 * r + i])

    w_across = remote(
        w_ref.at[pl.ds(pl.multiple_of((py + 2 * jy) * 128, 128), 128)], wr.at[1, jy, zl],
        w_send.at[12], w_recv.at[12], device(2, 0, 0, 0),
    )

    def w_other_half(q):
        if q < 2:
            w_arrived(1, q)
            copy = remote(
                wr.at[0, jn, blocks[q]], wr.at[1, jn, blocks[q]],
                w_send.at[13 + q], w_recv.at[13 + q], device(2, 0, 0, 0),
            )
        else:
            w_arrived(2, q)
            ref = wr.at[1, jy, blocks[q]]
            copy = remote(ref, ref, w_send.at[13 + q], w_recv.at[13 + q], device(0, 2, 0, 0))
        copy.start()
        w_copies.append(copy)

    k_copies = []
    for i, (dx, dy, row, rows, slot) in enumerate(DIRS):
        copy = remote(
            kr.at[pl.ds(row, rows)], kr.at[pl.ds(slot, rows)], k_send.at[i], k_recv.at[i], device(dx, dy, 0, 0)
        )
        copy.start()
        k_copies.append(copy)
    k_own = remote(
        kr.at[pl.ds(0, ROWS)], kr.at[pl.ds(512, ROWS)], k_send.at[8], k_recv.at[8], device(0, 0, 0, 1)
    )
    k_own.start()
    x_copies = ([], [])
    staged = set()
    for o in range(2):
        if o == 0:
            w_across.start()
            w_copies.append(w_across)
            w_along_z(0)
        for i, (dx, dy, dc, row, rows, slot, rel) in enumerate(ITEMS):
            if rel not in staged:
                staged.add(rel)
                landed(xs.at[rel - 1], stage_sem.at[rel])
            there = lax.div(lax.rem(y + dy + 4, 4), 2)
            copy = remote(
                xs.at[rel - 1, there if o else 1 - there, pl.ds(row, rows)],
                xr.at[o, pl.ds(slot, rows)],
                x_send.at[o, i], x_recv.at[o, i], device(dx, dy, 0, dc),
            )
            copy.start()
            x_copies[o].append(copy)
    landed(xr.at[:, pl.ds(0, ROWS)], stage_sem.at[0])

    for copy in k_copies:
        copy.wait_recv()
    relay = remote(
        kr.at[pl.ds(128, 384)], kr.at[pl.ds(640, 384)], k_send.at[9], k_recv.at[9], device(0, 0, 0, 1)
    )
    relay.start()
    k_own.wait_recv()
    own_kind = lax.div(x, 2).astype(F32)

    def masked(i):
        rows = pl.ds(i * 128, 128)
        mask = (1.0 - jnp.abs(kr[rows, KV:].astype(F32) - own_kind)).astype(BF16)
        values = kr[rows, 0:KV]
        own = values * jnp.concatenate([mask] * 4, 1)
        k2[rows, 0:KV] = own
        k2[rows, KV:] = values - own

    for i in range(5):
        masked(i)
    relay.wait_recv()
    for i in range(5, 8):
        masked(i)
    w_across.wait_recv()
    w_along_z(2)
    w_along_z(1)

    def partial(o):
        for copy in x_copies[o]:
            copy.wait_recv()
        for half in range(2):
            lanes = pl.ds(half * KV, KV)
            value = lax.dot_general(
                xr[o], k2[:, lanes], (((0,), (0,)), ((), ())), preferred_element_type=F32
            )
            part[o, :, :, :, lanes] = value.reshape(ZL, ZH, 32, KV)

    dims = (((1,), (1,)), ((), ()))

    def send_back(n, j, first, last, lanes):
        for i, (dx, dy, dc, row, rows, slot, rel) in enumerate(ITEMS):
            if first <= slot < last:
                copy = remote(
                    dxs.at[j, pl.ds(slot, rows), lanes], dxr.at[rel - 1, j, pl.ds(row, rows), lanes],
                    d_send.at[n, i], d_recv.at[n, i], device(-dx, -dy, 0, dc),
                )
                copy.start()
                d_copies.append(copy)

    def state_grad(block):
        if block == 0:
            for q in range(4):
                w_arrived(0, q)
            for q in range(2):
                w_arrived(2, q)
        rows = pl.ds(block * 256, 256)
        own, other = wr[0, jy].reshape(512, KV), wr[1, jy].reshape(512, KV)
        value = lax.dot_general(k2[rows, 0:KV], own, dims, preferred_element_type=F32)
        value += lax.dot_general(k2[rows, KV:], other, dims, preferred_element_type=F32)
        dxs[jy, rows] = value.astype(BF16)
        send_back(0, jy, block * 256, block * 256 + 256, pl.ds(0, KV))

    def state_grad_late(q):
        if q > 1:
            w_arrived(1, q)
        landed(wr.at[1, jn, blocks[q]], w_recv.at[13 + q])
        lanes = pl.ds(pl.multiple_of(blocks[q] * 128, 128), 128)
        for block in range(2):
            rows = pl.ds(block * 512, 512)
            value = lax.dot_general(k2[rows, 0:KV], wr[0, jn, blocks[q]], dims, preferred_element_type=F32)
            value += lax.dot_general(k2[rows, KV:], wr[1, jn, blocks[q]], dims, preferred_element_type=F32)
            dxs[jn, rows, lanes] = value.astype(BF16)
        send_back(1 + q, jn, 0, GROUP, lanes)

    def chunk(target):
        target = lax.rem(target + NZ, NZ)
        return lax.rem(target, 4), lax.div(target, 4)

    def chain(step, o, half):
        rows = pl.ds(half * UNIT, UNIT)
        for at, (dz, target, count) in enumerate(((-1, z + 8 + step, 8), (1, z + 7 - step, 7))):
            if step >= count:
                continue
            if step > 0:
                for copy in chains[step - 1, o, half, at]:
                    copy.wait_recv()
            l, h = chunk(target)
            codes, scale = sums.at[at, step, o, half], units.at[at, step, o, half]
            value = part[o, l, h, rows]
            if step > 0:
                value += codes[...].astype(F32) * scale[0:1, 0:1]
            top = jnp.maximum(jnp.max(jnp.abs(value), keepdims=True), 1e-30)
            codes[...] = jnp.round(value * (TOP / top)).astype(I32).astype(I16)
            scale[...] = jnp.broadcast_to(top * (1.0 / TOP), (8, 128))
            to, copies = device(0, 0, dz, 0), []
            for i, ref in enumerate((units, sums)):
                copy = remote(
                    ref.at[at, step, o, half], ref.at[at, step + 1, o, half],
                    c_send.at[at, step, o, half, i], c_recv.at[at, step, o, half, i], to,
                )
                copy.start()
                copies.append(copy)
            chains[step, o, half, at] = copies

    partial(0)
    for half in range(2):
        chain(0, 0, half)
    partial(1)
    for half in range(2):
        chain(0, 1, half)
    for q in range(4):
        w_other_half(q)

    background = {
        (1, 0): lambda: state_grad(0),
        (1, 1): lambda: state_grad(1),
        (1, 2): lambda: state_grad(2),
        (1, 3): lambda: state_grad(3),
        (2, 3): lambda: state_grad_late(0),
        (3, 3): lambda: state_grad_late(1),
        (4, 3): lambda: state_grad_late(2),
        (5, 3): lambda: state_grad_late(3),
    }
    for step in range(1, 8):
        for unit in range(4):
            chain(step, unit // 2, unit % 2)
            if (step, unit) in background:
                background[step, unit]()

    l_copies = []
    for o in range(2):
        for half in range(2):
            rows = pl.ds(half * UNIT, UNIT)
            value = part[o, zl, zh, rows]
            for at, count in ((0, 8), (1, 7)):
                for copy in chains[count - 1, o, half, at]:
                    copy.wait_recv()
                value += sums[at, count, o, half].astype(F32) * units[at, count, o, half, 0:1, 0:1]
            total[o, rows] = value
        for i, dx, dy, first in (((0, 2, 2, KV), (1, 0, 2, 0)), ((2, 2, 0, KV),))[o]:
            copy = remote(
                total.at[o, :, pl.ds(first, KV)], last.at[i], l_send.at[i], l_recv.at[i], device(dx, dy, 0, 0)
            )
            copy.start()
            l_copies.append(copy)

    for copy in d_copies:
        copy.wait_recv()
    for rel in range(8):
        for l in range(ZL):
            for j in range(2):
                lanes = pl.ds(l * 128, 128)
                src = dxs.at[j, pl.ds(0, ROWS), lanes] if rel == 0 else dxr.at[rel - 1, j, :, lanes]
                pltpu.make_async_copy(src, dx_ref.at[:, pl.ds(column(rel, l, j), 128)], out_sem.at[0]).start()
    for copy in l_copies:
        copy.wait_recv()
    dw_ref[...] = (total[1, :, 0:KV] + last[0] + last[1] + last[2]) * (1.0 / 256.0)

    landed(dx_ref, out_sem.at[0])
    for copy in k_copies + [k_own, relay] + x_copies[0] + x_copies[1] + w_copies:
        copy.wait_send()
    for copy in d_copies + l_copies:
        copy.wait_send()
    for copies in chains.values():
        for copy in copies:
            copy.wait_send()


def body(normed_states, kv_cotangent, token_types, kv_weight):
    any_spec, vmem = pl.BlockSpec(memory_space=pl.ANY), pl.BlockSpec(memory_space=pltpu.VMEM)
    dma = pltpu.SemaphoreType.DMA
    return pl.pallas_call(
        kernel,
        out_shape=(
            pltpu.VMEM((ROWS, WIDTH), BF16),
            jax.ShapeDtypeStruct((32, KV), F32),
        ),
        in_specs=[any_spec] * 4,
        out_specs=(vmem, vmem),
        scratch_shapes=[
            pltpu.VMEM((7, 2, ROWS, KV), BF16),
            pltpu.VMEM((2, GROUP, KV), BF16),
            pltpu.VMEM((GROUP, KV + 128), BF16),
            pltpu.VMEM((GROUP, 2 * KV), BF16),
            pltpu.VMEM((1, ROWS), I32),
            pltpu.VMEM((2, 2, ZL, 128, KV), BF16),
            pltpu.VMEM((2, ZL, ZH, 32, 2 * KV), F32),
            pltpu.VMEM((2, 9, 2, 2, UNIT, 2 * KV), I16),
            pltpu.VMEM((2, 9, 2, 2, 8, 128), F32),
            pltpu.VMEM((2, GROUP, KV), BF16),
            pltpu.VMEM((7, 2, ROWS, KV), BF16),
            pltpu.VMEM((3, 32, KV), F32),
            pltpu.VMEM((2, 32, 2 * KV), F32),
            dma((8,)),
            dma((2, len(ITEMS))),
            dma((2, len(ITEMS))),
            dma((10,)),
            dma((10,)),
            dma((17,)),
            dma((17,)),
            dma((5, len(ITEMS))),
            dma((5, len(ITEMS))),
            dma((2, 8, 2, 2, 2)),
            dma((2, 8, 2, 2, 2)),
            dma((3,)),
            dma((3,)),
            dma((4,)),
            dma((1,)),
        ],
        compiler_params=pltpu.CompilerParams(
            collective_id=0, has_side_effects=True, vmem_limit_bytes=60 * 2**20
        ),
        cost_estimate=pl.CostEstimate(flops=2**32, bytes_accessed=5 * 2**20, transcendentals=0),
        name="exchange",
    )(normed_states, kv_cotangent, token_types.reshape(1, ROWS), kv_weight)


def solution(mesh):
    in_specs = (
        P(("dp", "mod"), None),
        P(("dp", "mod"), None),
        P(("dp", "mod"), None),
        P("mod", None),
    )
    out_specs = (P(("dp", "mod"), None), P(("mod", "dp"), None))
    return jax.shard_map(body, mesh=mesh, in_specs=in_specs, out_specs=out_specs, check_vma=False)
```

```python
import jax
import jax.numpy as jnp
from jax import lax
from jax.experimental import pallas as pl
from jax.experimental.pallas import tpu as pltpu
from jax.sharding import PartitionSpec as P

MESH = pl.DeviceIdType.MESH
F32, BF16, I16, I32 = jnp.float32, jnp.bfloat16, jnp.int16, jnp.int32
ROWS, WIDTH, KV = 128, 8192, 512
HALF, QUARTER = ROWS // 2, ROWS // 4
GROUP = 8 * ROWS
ZL, ZH, NZ = 4, 4, 16
UNIT = 16
TOP = 32767.0

DIRS = (
    (1, 0, 0, HALF, 128),
    (-1, 0, HALF, HALF, 192),
    (0, 1, 0, HALF, 256),
    (0, -1, HALF, HALF, 320),
    (1, 1, 0, QUARTER, 384),
    (1, -1, QUARTER, QUARTER, 416),
    (-1, 1, 2 * QUARTER, QUARTER, 448),
    (-1, -1, 3 * QUARTER, QUARTER, 480),
)
ITEMS = tuple(
    (dx, dy, dc, row, rows, dc * 512 + slot, abs(dx) * 4 + abs(dy) * 2 + dc)
    for dx, dy, row, rows, slot in DIRS
    for dc in (0, 1)
) + ((0, 0, 1, 0, ROWS, 512, 1),)
ALONG_Z = ((1, 0, 128, 1), (-1, 0, 128, 2), (2, 0, 64, 3), (-2, 64, 64, 3))


def kernel(
    x_ref, k_ref, t_ref, w_ref, dx_ref, dw_ref,
    xs, xr, kr, k2, kinds, wr, part, sums, units, dxs, dxr, last, total,
    stage_sem, x_send, x_recv, k_send, k_recv, w_send, w_recv, d_send, d_recv,
    c_send, c_recv, l_send, l_recv, local_sem, out_sem,
):
    dp, mod = lax.axis_index("dp"), lax.axis_index("mod")
    y, zh = lax.div(dp, 4), lax.rem(dp, 4)
    x, zl, c = lax.div(mod, 8), lax.rem(lax.div(mod, 2), 4), lax.rem(mod, 2)
    z = zh * 4 + zl
    px, py, jy = lax.rem(x, 2), lax.rem(y, 2), lax.div(y, 2)
    jn = 1 - jy

    def device(dx, dy, dz, dc):
        xx, yy = lax.rem(x + dx + 4, 4), lax.rem(y + dy + 4, 4)
        zz, cc = lax.rem(z + dz + NZ, NZ), lax.rem(c + dc, 2)
        return (yy * 4 + lax.div(zz, 4), xx * 8 + lax.rem(zz, 4) * 2 + cc)

    def column(rel, l, j):
        xx, yy = lax.rem(px + rel // 4, 2), lax.rem(py + (rel // 2) % 2, 2)
        cc = lax.rem(c + rel % 2, 2)
        return pl.multiple_of(xx * 4096 + l * 1024 + cc * 512 + yy * 128 + j * 256, 128)

    def remote(src, dst, send, recv, to):
        return pltpu.make_async_remote_copy(
            src_ref=src, dst_ref=dst, send_sem=send, recv_sem=recv,
            device_id=to, device_id_type=MESH,
        )

    def landed(ref, sem):
        pltpu.make_async_copy(ref, ref, sem).wait()

    barrier = pltpu.get_barrier_semaphore()
    greeted = [(dx, dy, 0, dc) for dx, dy, dc, *_ in ITEMS]
    greeted += [(0, 0, 1, 0), (0, 0, -1, 0), (0, 0, 2, 0), (0, 0, -2, 0)]
    greeted += [(2, 0, 0, 0), (0, 2, 0, 0), (2, 2, 0, 0)]
    for offsets in greeted:
        pl.semaphore_signal(barrier, inc=1, device_id=device(*offsets), device_id_type=MESH)

    k_in = pltpu.make_async_copy(k_ref, kr.at[pl.ds(0, ROWS), pl.ds(0, KV)], local_sem.at[0])
    k_in.start()
    t_in = pltpu.make_async_copy(t_ref, kinds, local_sem.at[1])
    t_in.start()
    for rel in (4, 5, 2, 3, 6, 7, 1):
        for l in range(ZL):
            for j in range(2):
                pltpu.make_async_copy(
                    x_ref.at[:, pl.ds(column(rel, l, j), 128)],
                    xs.at[rel - 1, j, :, pl.ds(l * 128, 128)],
                    stage_sem.at[rel],
                ).start()
    for o, j in enumerate((jn, jy)):
        for l in range(ZL):
            pltpu.make_async_copy(
                x_ref.at[:, pl.ds(column(0, l, j), 128)],
                xr.at[o, pl.ds(0, ROWS), pl.ds(l * 128, 128)],
                stage_sem.at[0],
            ).start()
    for r, j in enumerate((jy, jn)):
        rows = pl.ds(pl.multiple_of((py + 2 * j) * 128, 128), 128)
        pltpu.make_async_copy(w_ref.at[rows], wr.at[0, j, zl], local_sem.at[2 + r]).start()
    k_in.wait()
    t_in.wait()
    kr[0:ROWS, KV:] = jnp.broadcast_to(kinds[...].astype(F32), (ROWS, 128)).T.astype(BF16)

    pl.semaphore_wait(barrier, len(greeted))

    w_copies, d_copies, chains = [], [], {}
    blocks = [lax.rem(zl + 4 + d, 4) for d in (0, -1, 1, 2)]

    def w_along_z(r):
        j = (jy, jn, jy)[r]
        for i, (dz, row, rows, _) in enumerate(ALONG_Z[:2] if r == 1 else ALONG_Z):
            start = pl.multiple_of((py + 2 * j) * 128 + row, 64)
            dst = wr.at[r // 2, j, zl, pl.ds(row, rows)]
            copy = remote(
                dst if r == 2 else w_ref.at[pl.ds(start, rows)], dst,
                w_send.at[4 * r + i], w_recv.at[4 * r + i], device(0, 0, dz, 0),
            )
            copy.start()
            w_copies.append(copy)

    def w_arrived(r, q):
        j = (jy, jn, jy)[r]
        if q == 0 and r < 2:
            landed(wr.at[0, j, zl], local_sem.at[2 + r])
        for i, (_, row, rows, place) in enumerate(ALONG_Z):
            if place == q:
                landed(wr.at[r // 2, j, blocks[q], pl.ds(row, rows)], w_recv.at[4 * r + i])

    w_across = remote(
        w_ref.at[pl.ds(pl.multiple_of((py + 2 * jy) * 128, 128), 128)], wr.at[1, jy, zl],
        w_send.at[12], w_recv.at[12], device(2, 0, 0, 0),
    )

    def w_other_half(q):
        if q == 3:
            w_arrived(0, q)
            ref = wr.at[0, jy, blocks[q]]
            copy = remote(ref, ref, w_send.at[17], w_recv.at[17], device(0, 2, 0, 0))
            copy.start()
            w_copies.append(copy)
        if q < 2:
            w_arrived(1, q)
            copy = remote(
                wr.at[0, jn, blocks[q]], wr.at[1, jn, blocks[q]],
                w_send.at[13 + q], w_recv.at[13 + q], device(2, 0, 0, 0),
            )
        else:
            w_arrived(2, q)
            ref = wr.at[1, jy, blocks[q]]
            copy = remote(ref, ref, w_send.at[13 + q], w_recv.at[13 + q], device(0, 2, 0, 0))
        copy.start()
        w_copies.append(copy)

    k_copies = []
    for i, (dx, dy, row, rows, slot) in enumerate(DIRS):
        copy = remote(
            kr.at[pl.ds(row, rows)], kr.at[pl.ds(slot, rows)], k_send.at[i], k_recv.at[i], device(dx, dy, 0, 0)
        )
        copy.start()
        k_copies.append(copy)
    k_own = remote(
        kr.at[pl.ds(0, ROWS)], kr.at[pl.ds(512, ROWS)], k_send.at[8], k_recv.at[8], device(0, 0, 0, 1)
    )
    k_own.start()
    x_copies = ([], [])
    staged = set()
    for o in range(2):
        if o == 0:
            w_across.start()
            w_copies.append(w_across)
            w_along_z(0)
        for i, (dx, dy, dc, row, rows, slot, rel) in enumerate(ITEMS):
            if rel not in staged:
                staged.add(rel)
                landed(xs.at[rel - 1], stage_sem.at[rel])
            there = lax.div(lax.rem(y + dy + 4, 4), 2)
            copy = remote(
                xs.at[rel - 1, there if o else 1 - there, pl.ds(row, rows)],
                xr.at[o, pl.ds(slot, rows)],
                x_send.at[o, i], x_recv.at[o, i], device(dx, dy, 0, dc),
            )
            copy.start()
            x_copies[o].append(copy)
    landed(xr.at[:, pl.ds(0, ROWS)], stage_sem.at[0])

    for copy in k_copies:
        copy.wait_recv()
    relay = remote(
        kr.at[pl.ds(128, 384)], kr.at[pl.ds(640, 384)], k_send.at[9], k_recv.at[9], device(0, 0, 0, 1)
    )
    relay.start()
    k_own.wait_recv()
    own_kind = lax.div(x, 2).astype(F32)

    def masked(i):
        rows = pl.ds(i * 128, 128)
        mask = (1.0 - jnp.abs(kr[rows, KV:].astype(F32) - own_kind)).astype(BF16)
        values = kr[rows, 0:KV]
        own = values * jnp.concatenate([mask] * 4, 1)
        k2[rows, 0:KV] = own
        k2[rows, KV:] = values - own

    for i in range(5):
        masked(i)
    relay.wait_recv()
    for i in range(5, 8):
        masked(i)
    w_across.wait_recv()
    w_along_z(2)
    w_along_z(1)

    def partial(o):
        for copy in x_copies[o]:
            copy.wait_recv()
        for half in range(2):
            lanes = pl.ds(half * KV, KV)
            value = lax.dot_general(
                xr[o], k2[:, lanes], (((0,), (0,)), ((), ())), preferred_element_type=F32
            )
            part[o, :, :, :, lanes] = value.reshape(ZL, ZH, 32, KV)

    dims = (((1,), (1,)), ((), ()))

    def send_back(n, j, first, last, lanes):
        for i, (dx, dy, dc, row, rows, slot, rel) in enumerate(ITEMS):
            if first <= slot < last:
                copy = remote(
                    dxs.at[j, pl.ds(slot, rows), lanes], dxr.at[rel - 1, j, pl.ds(row, rows), lanes],
                    d_send.at[n, i], d_recv.at[n, i], device(-dx, -dy, 0, dc),
                )
                copy.start()
                d_copies.append(copy)

    def state_grad(block):
        if block == 0:
            for q in range(3):
                w_arrived(0, q)
            for q in range(2):
                w_arrived(2, q)
        rows = pl.ds(block * 256, 256)
        own, other = wr[0, jy].reshape(512, KV), wr[1, jy].reshape(512, KV)
        value = lax.dot_general(k2[rows, 0:KV], own, dims, preferred_element_type=F32)
        value += lax.dot_general(k2[rows, KV:], other, dims, preferred_element_type=F32)
        dxs[jy, rows] = value.astype(BF16)
        send_back(0, jy, block * 256, block * 256 + 256, pl.ds(0, KV))

    def state_grad_late(q):
        if q == 2:
            w_arrived(1, q)
        if q == 3:
            landed(wr.at[0, jn, blocks[q]], w_recv.at[17])
        landed(wr.at[1, jn, blocks[q]], w_recv.at[13 + q])
        lanes = pl.ds(pl.multiple_of(blocks[q] * 128, 128), 128)
        for block in range(2):
            rows = pl.ds(block * 512, 512)
            value = lax.dot_general(k2[rows, 0:KV], wr[0, jn, blocks[q]], dims, preferred_element_type=F32)
            value += lax.dot_general(k2[rows, KV:], wr[1, jn, blocks[q]], dims, preferred_element_type=F32)
            dxs[jn, rows, lanes] = value.astype(BF16)
        send_back(1 + q, jn, 0, GROUP, lanes)

    def chunk(target):
        target = lax.rem(target + NZ, NZ)
        return lax.rem(target, 4), lax.div(target, 4)

    def chain(step, o, half):
        rows = pl.ds(half * UNIT, UNIT)
        for at, (dz, target, count) in enumerate(((-1, z + 8 + step, 8), (1, z + 7 - step, 7))):
            if step >= count:
                continue
            if step > 0:
                for copy in chains[step - 1, o, half, at]:
                    copy.wait_recv()
            l, h = chunk(target)
            codes, scale = sums.at[at, step, o, half], units.at[at, step, o, half]
            value = part[o, l, h, rows]
            if step > 0:
                value += codes[...].astype(F32) * scale[0:1, 0:1]
            top = jnp.maximum(jnp.max(jnp.abs(value), keepdims=True), 1e-30)
            codes[...] = jnp.round(value * (TOP / top)).astype(I32).astype(I16)
            scale[...] = jnp.broadcast_to(top * (1.0 / TOP), (1, 128))
            to, copies = device(0, 0, dz, 0), []
            for i, ref in enumerate((units, sums)):
                copy = remote(
                    ref.at[at, step, o, half], ref.at[at, step + 1, o, half],
                    c_send.at[at, step, o, half, i], c_recv.at[at, step, o, half, i], to,
                )
                copy.start()
                copies.append(copy)
            chains[step, o, half, at] = copies

    partial(0)
    for half in range(2):
        chain(0, 0, half)
    partial(1)
    for half in range(2):
        chain(0, 1, half)
    for q in range(4):
        w_other_half(q)

    background = {
        (1, 0): lambda: state_grad(0),
        (1, 1): lambda: state_grad(1),
        (1, 2): lambda: state_grad(2),
        (1, 3): lambda: state_grad(3),
        (2, 3): lambda: state_grad_late(0),
        (3, 3): lambda: state_grad_late(1),
        (4, 3): lambda: state_grad_late(2),
        (5, 3): lambda: state_grad_late(3),
    }
    for step in range(1, 8):
        for unit in range(4):
            chain(step, unit // 2, unit % 2)
            if (step, unit) in background:
                background[step, unit]()

    l_copies = []
    for o in range(2):
        for half in range(2):
            rows = pl.ds(half * UNIT, UNIT)
            value = part[o, zl, zh, rows]
            for at, count in ((0, 8), (1, 7)):
                for copy in chains[count - 1, o, half, at]:
                    copy.wait_recv()
                value += sums[at, count, o, half].astype(F32) * units[at, count, o, half, 0:1, 0:1]
            total[o, rows] = value
        for i, dx, dy, first in (((0, 2, 2, KV), (1, 0, 2, 0)), ((2, 2, 0, KV),))[o]:
            copy = remote(
                total.at[o, :, pl.ds(first, KV)], last.at[i], l_send.at[i], l_recv.at[i], device(dx, dy, 0, 0)
            )
            copy.start()
            l_copies.append(copy)

    for copy in d_copies:
        copy.wait_recv()
    for rel in range(8):
        for l in range(ZL):
            for j in range(2):
                lanes = pl.ds(l * 128, 128)
                src = dxs.at[j, pl.ds(0, ROWS), lanes] if rel == 0 else dxr.at[rel - 1, j, :, lanes]
                pltpu.make_async_copy(src, dx_ref.at[:, pl.ds(column(rel, l, j), 128)], out_sem.at[0]).start()
    for copy in l_copies:
        copy.wait_recv()
    dw_ref[...] = (total[1, :, 0:KV] + last[0] + last[1] + last[2]) * (1.0 / 256.0)

    landed(dx_ref, out_sem.at[0])
    for copy in k_copies + [k_own, relay] + x_copies[0] + x_copies[1] + w_copies:
        copy.wait_send()
    for copy in d_copies + l_copies:
        copy.wait_send()
    for copies in chains.values():
        for copy in copies:
            copy.wait_send()


def body(normed_states, kv_cotangent, token_types, kv_weight):
    any_spec, vmem = pl.BlockSpec(memory_space=pl.ANY), pl.BlockSpec(memory_space=pltpu.VMEM)
    dma = pltpu.SemaphoreType.DMA
    return pl.pallas_call(
        kernel,
        out_shape=(
            pltpu.VMEM((ROWS, WIDTH), BF16),
            jax.ShapeDtypeStruct((32, KV), F32),
        ),
        in_specs=[any_spec] * 4,
        out_specs=(vmem, vmem),
        scratch_shapes=[
            pltpu.VMEM((7, 2, ROWS, KV), BF16),
            pltpu.VMEM((2, GROUP, KV), BF16),
            pltpu.VMEM((GROUP, KV + 128), BF16),
            pltpu.VMEM((GROUP, 2 * KV), BF16),
            pltpu.VMEM((1, ROWS), I32),
            pltpu.VMEM((2, 2, ZL, 128, KV), BF16),
            pltpu.VMEM((2, ZL, ZH, 32, 2 * KV), F32),
            pltpu.VMEM((2, 9, 2, 2, UNIT, 2 * KV), I16),
            pltpu.VMEM((2, 9, 2, 2, 1, 128), F32),
            pltpu.VMEM((2, GROUP, KV), BF16),
            pltpu.VMEM((7, 2, ROWS, KV), BF16),
            pltpu.VMEM((3, 32, KV), F32),
            pltpu.VMEM((2, 32, 2 * KV), F32),
            dma((8,)),
            dma((2, len(ITEMS))),
            dma((2, len(ITEMS))),
            dma((10,)),
            dma((10,)),
            dma((18,)),
            dma((18,)),
            dma((5, len(ITEMS))),
            dma((5, len(ITEMS))),
            dma((2, 8, 2, 2, 2)),
            dma((2, 8, 2, 2, 2)),
            dma((3,)),
            dma((3,)),
            dma((4,)),
            dma((1,)),
        ],
        compiler_params=pltpu.CompilerParams(
            collective_id=0, has_side_effects=True, vmem_limit_bytes=60 * 2**20
        ),
        cost_estimate=pl.CostEstimate(flops=2**32, bytes_accessed=5 * 2**20, transcendentals=0),
        name="exchange",
    )(normed_states, kv_cotangent, token_types.reshape(1, ROWS), kv_weight)


def solution(mesh):
    in_specs = (
        P(("dp", "mod"), None),
        P(("dp", "mod"), None),
        P(("dp", "mod"), None),
        P("mod", None),
    )
    out_specs = (P(("dp", "mod"), None), P(("mod", "dp"), None))
    return jax.shard_map(body, mesh=mesh, in_specs=in_specs, out_specs=out_specs, check_vma=False)
```

```python
import jax
import jax.numpy as jnp
from jax import lax
from jax.experimental import pallas as pl
from jax.experimental.pallas import tpu as pltpu
from jax.sharding import PartitionSpec as P

MESH = pl.DeviceIdType.MESH
F32, BF16, I16, I32 = jnp.float32, jnp.bfloat16, jnp.int16, jnp.int32
ROWS, WIDTH, KV = 128, 8192, 512
HALF, QUARTER = ROWS // 2, ROWS // 4
GROUP = 8 * ROWS
ZL, ZH, NZ = 4, 4, 16
UNIT = 16
TOP = 32767.0

DIRS = (
    (1, 0, 0, HALF, 128),
    (-1, 0, HALF, HALF, 192),
    (0, 1, 0, HALF, 256),
    (0, -1, HALF, HALF, 320),
    (1, 1, 0, QUARTER, 384),
    (1, -1, QUARTER, QUARTER, 416),
    (-1, 1, 2 * QUARTER, QUARTER, 448),
    (-1, -1, 3 * QUARTER, QUARTER, 480),
)
ITEMS = tuple(
    (dx, dy, dc, row, rows, dc * 512 + slot, abs(dx) * 4 + abs(dy) * 2 + dc)
    for dx, dy, row, rows, slot in DIRS
    for dc in (0, 1)
) + ((0, 0, 1, 0, ROWS, 512, 1),)
ALONG_Z = ((1, 0, 128, 1), (-1, 0, 128, 2), (2, 0, 64, 3), (-2, 64, 64, 3))


def kernel(
    x_ref, k_ref, t_ref, w_ref, dx_ref, dw_ref,
    xs, xr, kr, k2, kinds, wr, part, sums, units, dxs, dxr, last, total,
    stage_sem, x_send, x_recv, k_send, k_recv, w_send, w_recv, d_send, d_recv,
    c_send, c_recv, l_send, l_recv, local_sem, out_sem,
):
    dp, mod = lax.axis_index("dp"), lax.axis_index("mod")
    y, zh = lax.div(dp, 4), lax.rem(dp, 4)
    x, zl, c = lax.div(mod, 8), lax.rem(lax.div(mod, 2), 4), lax.rem(mod, 2)
    z = zh * 4 + zl
    px, py, jy = lax.rem(x, 2), lax.rem(y, 2), lax.div(y, 2)
    jn = 1 - jy

    def device(dx, dy, dz, dc):
        xx, yy = lax.rem(x + dx + 4, 4), lax.rem(y + dy + 4, 4)
        zz, cc = lax.rem(z + dz + NZ, NZ), lax.rem(c + dc, 2)
        return (yy * 4 + lax.div(zz, 4), xx * 8 + lax.rem(zz, 4) * 2 + cc)

    def column(rel, l, j):
        xx, yy = lax.rem(px + rel // 4, 2), lax.rem(py + (rel // 2) % 2, 2)
        cc = lax.rem(c + rel % 2, 2)
        return pl.multiple_of(xx * 4096 + l * 1024 + cc * 512 + yy * 128 + j * 256, 128)

    def remote(src, dst, send, recv, to):
        return pltpu.make_async_remote_copy(
            src_ref=src, dst_ref=dst, send_sem=send, recv_sem=recv,
            device_id=to, device_id_type=MESH,
        )

    def landed(ref, sem):
        pltpu.make_async_copy(ref, ref, sem).wait()

    barrier = pltpu.get_barrier_semaphore()
    greeted = [(dx, dy, 0, dc) for dx, dy, dc, *_ in ITEMS]
    greeted += [(0, 0, 1, 0), (0, 0, -1, 0), (0, 0, 2, 0), (0, 0, -2, 0)]
    greeted += [(2, 0, 0, 0), (0, 2, 0, 0), (2, 2, 0, 0)]
    for offsets in greeted:
        pl.semaphore_signal(barrier, inc=1, device_id=device(*offsets), device_id_type=MESH)

    k_in = pltpu.make_async_copy(k_ref, kr.at[pl.ds(0, ROWS), pl.ds(0, KV)], local_sem.at[0])
    k_in.start()
    t_in = pltpu.make_async_copy(t_ref, kinds, local_sem.at[1])
    t_in.start()
    for rel in (4, 5, 2, 3, 6, 7, 1):
        for l in range(ZL):
            for j in range(2):
                pltpu.make_async_copy(
                    x_ref.at[:, pl.ds(column(rel, l, j), 128)],
                    xs.at[rel - 1, j, :, pl.ds(l * 128, 128)],
                    stage_sem.at[rel],
                ).start()
    for o, j in enumerate((jn, jy)):
        for l in range(ZL):
            pltpu.make_async_copy(
                x_ref.at[:, pl.ds(column(0, l, j), 128)],
                xr.at[o, pl.ds(0, ROWS), pl.ds(l * 128, 128)],
                stage_sem.at[0],
            ).start()
    for r, j in enumerate((jy, jn)):
        rows = pl.ds(pl.multiple_of((py + 2 * j) * 128, 128), 128)
        pltpu.make_async_copy(w_ref.at[rows], wr.at[0, j, zl], local_sem.at[2 + r]).start()
    k_in.wait()
    t_in.wait()
    kr[0:ROWS, KV:] = jnp.broadcast_to(kinds[...].astype(F32), (ROWS, 128)).T.astype(BF16)

    pl.semaphore_wait(barrier, len(greeted))

    w_copies, d_copies, chains = [], [], {}
    blocks = [lax.rem(zl + 4 + d, 4) for d in (0, -1, 1, 2)]

    def w_along_z(r):
        j = (jy, jn, jy)[r]
        for i, (dz, row, rows, _) in enumerate(ALONG_Z[:2] if r == 1 else ALONG_Z):
            start = pl.multiple_of((py + 2 * j) * 128 + row, 64)
            dst = wr.at[r // 2, j, zl, pl.ds(row, rows)]
            copy = remote(
                dst if r == 2 else w_ref.at[pl.ds(start, rows)], dst,
                w_send.at[4 * r + i], w_recv.at[4 * r + i], device(0, 0, dz, 0),
            )
            copy.start()
            w_copies.append(copy)

    def w_arrived(r, q):
        j = (jy, jn, jy)[r]
        if q == 0 and r < 2:
            landed(wr.at[0, j, zl], local_sem.at[2 + r])
        for i, (_, row, rows, place) in enumerate(ALONG_Z):
            if place == q:
                landed(wr.at[r // 2, j, blocks[q], pl.ds(row, rows)], w_recv.at[4 * r + i])

    w_across = remote(
        w_ref.at[pl.ds(pl.multiple_of((py + 2 * jy) * 128, 128), 128)], wr.at[1, jy, zl],
        w_send.at[12], w_recv.at[12], device(2, 0, 0, 0),
    )

    def w_other_half(q):
        if q == 3:
            w_arrived(0, q)
            ref = wr.at[0, jy, blocks[q]]
            copy = remote(ref, ref, w_send.at[17], w_recv.at[17], device(0, 2, 0, 0))
            copy.start()
            w_copies.append(copy)
        if q < 2:
            w_arrived(1, q)
            copy = remote(
                wr.at[0, jn, blocks[q]], wr.at[1, jn, blocks[q]],
                w_send.at[13 + q], w_recv.at[13 + q], device(2, 0, 0, 0),
            )
        else:
            w_arrived(2, q)
            ref = wr.at[1, jy, blocks[q]]
            copy = remote(ref, ref, w_send.at[13 + q], w_recv.at[13 + q], device(0, 2, 0, 0))
        copy.start()
        w_copies.append(copy)

    w_across.start()
    w_copies.append(w_across)
    w_along_z(0)
    k_copies = []
    for i, (dx, dy, row, rows, slot) in enumerate(DIRS):
        copy = remote(
            kr.at[pl.ds(row, rows)], kr.at[pl.ds(slot, rows)], k_send.at[i], k_recv.at[i], device(dx, dy, 0, 0)
        )
        copy.start()
        k_copies.append(copy)
    k_own = remote(
        kr.at[pl.ds(0, ROWS)], kr.at[pl.ds(512, ROWS)], k_send.at[8], k_recv.at[8], device(0, 0, 0, 1)
    )
    k_own.start()
    x_copies = ([], [])
    staged = set()
    for o in range(2):
        for i, (dx, dy, dc, row, rows, slot, rel) in enumerate(ITEMS):
            if rel not in staged:
                staged.add(rel)
                landed(xs.at[rel - 1], stage_sem.at[rel])
            there = lax.div(lax.rem(y + dy + 4, 4), 2)
            copy = remote(
                xs.at[rel - 1, there if o else 1 - there, pl.ds(row, rows)],
                xr.at[o, pl.ds(slot, rows)],
                x_send.at[o, i], x_recv.at[o, i], device(dx, dy, 0, dc),
            )
            copy.start()
            x_copies[o].append(copy)
    landed(xr.at[:, pl.ds(0, ROWS)], stage_sem.at[0])

    for copy in k_copies:
        copy.wait_recv()
    relay = remote(
        kr.at[pl.ds(128, 384)], kr.at[pl.ds(640, 384)], k_send.at[9], k_recv.at[9], device(0, 0, 0, 1)
    )
    relay.start()
    w_across.wait_recv()
    w_along_z(2)
    w_along_z(1)
    k_own.wait_recv()
    own_kind = lax.div(x, 2).astype(F32)

    def masked(i):
        rows = pl.ds(i * 128, 128)
        mask = (1.0 - jnp.abs(kr[rows, KV:].astype(F32) - own_kind)).astype(BF16)
        values = kr[rows, 0:KV]
        own = values * jnp.concatenate([mask] * 4, 1)
        k2[rows, 0:KV] = own
        k2[rows, KV:] = values - own

    for i in range(5):
        masked(i)
    relay.wait_recv()
    for i in range(5, 8):
        masked(i)

    def partial(o):
        for copy in x_copies[o]:
            copy.wait_recv()
        for half in range(2):
            lanes = pl.ds(half * KV, KV)
            value = lax.dot_general(
                xr[o], k2[:, lanes], (((0,), (0,)), ((), ())), preferred_element_type=F32
            )
            part[o, :, :, :, lanes] = value.reshape(ZL, ZH, 32, KV)

    dims = (((1,), (1,)), ((), ()))

    def send_back(n, j, first, last, lanes):
        for i, (dx, dy, dc, row, rows, slot, rel) in enumerate(ITEMS):
            if first <= slot < last:
                copy = remote(
                    dxs.at[j, pl.ds(slot, rows), lanes], dxr.at[rel - 1, j, pl.ds(row, rows), lanes],
                    d_send.at[n, i], d_recv.at[n, i], device(-dx, -dy, 0, dc),
                )
                copy.start()
                d_copies.append(copy)

    def state_grad(block):
        if block == 0:
            for q in range(3):
                w_arrived(0, q)
            for q in range(2):
                w_arrived(2, q)
        rows = pl.ds(block * 256, 256)
        own, other = wr[0, jy].reshape(512, KV), wr[1, jy].reshape(512, KV)
        value = lax.dot_general(k2[rows, 0:KV], own, dims, preferred_element_type=F32)
        value += lax.dot_general(k2[rows, KV:], other, dims, preferred_element_type=F32)
        dxs[jy, rows] = value.astype(BF16)
        send_back(0, jy, block * 256, block * 256 + 256, pl.ds(0, KV))

    def state_grad_late(q):
        if q == 2:
            w_arrived(1, q)
        if q == 3:
            landed(wr.at[0, jn, blocks[q]], w_recv.at[17])
        landed(wr.at[1, jn, blocks[q]], w_recv.at[13 + q])
        lanes = pl.ds(pl.multiple_of(blocks[q] * 128, 128), 128)
        for block in range(2):
            rows = pl.ds(block * 512, 512)
            value = lax.dot_general(k2[rows, 0:KV], wr[0, jn, blocks[q]], dims, preferred_element_type=F32)
            value += lax.dot_general(k2[rows, KV:], wr[1, jn, blocks[q]], dims, preferred_element_type=F32)
            dxs[jn, rows, lanes] = value.astype(BF16)
        send_back(1 + q, jn, 0, GROUP, lanes)

    def chunk(target):
        target = lax.rem(target + NZ, NZ)
        return lax.rem(target, 4), lax.div(target, 4)

    def chain(step, o, half):
        rows = pl.ds(half * UNIT, UNIT)
        for at, (dz, target, count) in enumerate(((-1, z + 8 + step, 8), (1, z + 7 - step, 7))):
            if step >= count:
                continue
            if step > 0:
                for copy in chains[step - 1, o, half, at]:
                    copy.wait_recv()
            l, h = chunk(target)
            codes, scale = sums.at[at, step, o, half], units.at[at, step, o, half]
            value = part[o, l, h, rows]
            if step > 0:
                value += codes[...].astype(F32) * scale[0:1, 0:1]
            top = jnp.maximum(jnp.max(jnp.abs(value), keepdims=True), 1e-30)
            codes[...] = jnp.round(value * (TOP / top)).astype(I32).astype(I16)
            scale[...] = jnp.broadcast_to(top * (1.0 / TOP), (1, 128))
            to, copies = device(0, 0, dz, 0), []
            for i, ref in enumerate((units, sums)):
                copy = remote(
                    ref.at[at, step, o, half], ref.at[at, step + 1, o, half],
                    c_send.at[at, step, o, half, i], c_recv.at[at, step, o, half, i], to,
                )
                copy.start()
                copies.append(copy)
            chains[step, o, half, at] = copies

    partial(0)
    for half in range(2):
        chain(0, 0, half)
    partial(1)
    for half in range(2):
        chain(0, 1, half)
    for q in range(4):
        w_other_half(q)

    background = {
        (1, 0): lambda: state_grad(0),
        (1, 1): lambda: state_grad(1),
        (1, 2): lambda: state_grad(2),
        (1, 3): lambda: state_grad(3),
        (2, 3): lambda: state_grad_late(0),
        (3, 3): lambda: state_grad_late(1),
        (4, 3): lambda: state_grad_late(2),
        (5, 3): lambda: state_grad_late(3),
    }
    for step in range(1, 8):
        for unit in range(4):
            chain(step, unit // 2, unit % 2)
            if (step, unit) in background:
                background[step, unit]()

    l_copies = []
    for o in range(2):
        for half in range(2):
            rows = pl.ds(half * UNIT, UNIT)
            value = part[o, zl, zh, rows]
            for at, count in ((0, 8), (1, 7)):
                for copy in chains[count - 1, o, half, at]:
                    copy.wait_recv()
                value += sums[at, count, o, half].astype(F32) * units[at, count, o, half, 0:1, 0:1]
            total[o, rows] = value
        for i, dx, dy, first in (((0, 2, 2, KV), (1, 0, 2, 0)), ((2, 2, 0, KV),))[o]:
            copy = remote(
                total.at[o, :, pl.ds(first, KV)], last.at[i], l_send.at[i], l_recv.at[i], device(dx, dy, 0, 0)
            )
            copy.start()
            l_copies.append(copy)

    for copy in d_copies:
        copy.wait_recv()
    for rel in range(8):
        for l in range(ZL):
            for j in range(2):
                lanes = pl.ds(l * 128, 128)
                src = dxs.at[j, pl.ds(0, ROWS), lanes] if rel == 0 else dxr.at[rel - 1, j, :, lanes]
                pltpu.make_async_copy(src, dx_ref.at[:, pl.ds(column(rel, l, j), 128)], out_sem.at[0]).start()
    for copy in l_copies:
        copy.wait_recv()
    dw_ref[...] = (total[1, :, 0:KV] + last[0] + last[1] + last[2]) * (1.0 / 256.0)

    landed(dx_ref, out_sem.at[0])
    for copy in k_copies + [k_own, relay] + x_copies[0] + x_copies[1] + w_copies:
        copy.wait_send()
    for copy in d_copies + l_copies:
        copy.wait_send()
    for copies in chains.values():
        for copy in copies:
            copy.wait_send()


def body(normed_states, kv_cotangent, token_types, kv_weight):
    any_spec, vmem = pl.BlockSpec(memory_space=pl.ANY), pl.BlockSpec(memory_space=pltpu.VMEM)
    dma = pltpu.SemaphoreType.DMA
    return pl.pallas_call(
        kernel,
        out_shape=(
            pltpu.VMEM((ROWS, WIDTH), BF16),
            jax.ShapeDtypeStruct((32, KV), F32),
        ),
        in_specs=[any_spec] * 4,
        out_specs=(vmem, vmem),
        scratch_shapes=[
            pltpu.VMEM((7, 2, ROWS, KV), BF16),
            pltpu.VMEM((2, GROUP, KV), BF16),
            pltpu.VMEM((GROUP, KV + 128), BF16),
            pltpu.VMEM((GROUP, 2 * KV), BF16),
            pltpu.VMEM((1, ROWS), I32),
            pltpu.VMEM((2, 2, ZL, 128, KV), BF16),
            pltpu.VMEM((2, ZL, ZH, 32, 2 * KV), F32),
            pltpu.VMEM((2, 9, 2, 2, UNIT, 2 * KV), I16),
            pltpu.VMEM((2, 9, 2, 2, 1, 128), F32),
            pltpu.VMEM((2, GROUP, KV), BF16),
            pltpu.VMEM((7, 2, ROWS, KV), BF16),
            pltpu.VMEM((3, 32, KV), F32),
            pltpu.VMEM((2, 32, 2 * KV), F32),
            dma((8,)),
            dma((2, len(ITEMS))),
            dma((2, len(ITEMS))),
            dma((10,)),
            dma((10,)),
            dma((18,)),
            dma((18,)),
            dma((5, len(ITEMS))),
            dma((5, len(ITEMS))),
            dma((2, 8, 2, 2, 2)),
            dma((2, 8, 2, 2, 2)),
            dma((3,)),
            dma((3,)),
            dma((4,)),
            dma((1,)),
        ],
        compiler_params=pltpu.CompilerParams(
            collective_id=0, has_side_effects=True, vmem_limit_bytes=60 * 2**20
        ),
        cost_estimate=pl.CostEstimate(flops=2**32, bytes_accessed=5 * 2**20, transcendentals=0),
        name="exchange",
    )(normed_states, kv_cotangent, token_types.reshape(1, ROWS), kv_weight)


def solution(mesh):
    in_specs = (
        P(("dp", "mod"), None),
        P(("dp", "mod"), None),
        P(("dp", "mod"), None),
        P("mod", None),
    )
    out_specs = (P(("dp", "mod"), None), P(("mod", "dp"), None))
    return jax.shard_map(body, mesh=mesh, in_specs=in_specs, out_specs=out_specs, check_vma=False)
```
